512 devices in a mesh: ctx: 16 (over z), exp: 32 (over y, x, core).
Axes of the slice: x: 4, y: 4, z: 16, core: 2. Of those that a mesh axis runs over, the one named last changes fastest.
Arguments:
- queries: bfloat16 [1024, 4096], P('ctx', 'exp'), may hold values from -36 to 36
- keys: bfloat16 [1024, 1024], P('ctx'), may hold values from -4 to 4
- values: bfloat16 [1024, 1024], P('ctx'), may hold values from -6 to 6
- out_proj: bfloat16 [4096, 4096], P('ctx', 'exp'), may hold values from -0.09375 to 0.09375
- residual_in: bfloat16 [1024, 4096], P('ctx', 'exp'), may hold values from -48 to 48
- norm_gain: float32 [4096], P('exp'), may hold values from 0.1 to 1.9
- routes: int32 [1024, 2], replicated, may hold values from 0 to 7, all different within a row; in each aligned block of 64 rows (0 to 63, 64 to 127, ...) at most 16 rows name the same one
- gate_wts: float32 [1024, 2], P('ctx'), may hold values from 0.2 to 1
- w_gate: bfloat16 [4096, 65536], P(None, ('exp', 'ctx')), may hold values from -0.09375 to 0.09375
- w_up: bfloat16 [4096, 65536], P(None, ('exp', 'ctx')), may hold values from -0.09375 to 0.09375
- w_down: bfloat16 [65536, 4096], P(('exp', 'ctx')), may hold values from -0.25 to 0.25
Outputs:
- residual_out: bfloat16 [1024, 4096], P('ctx', 'exp')
- expert_out: bfloat16 [1024, 4096], P('ctx', 'exp')
The draws below stay inside these ranges and needn't reach their ends.
Inputs may be any that keep to these rules, and one draw needn't show every extreme that they name: `routes`: within the 64 tokens of one ctx shard no expert is named more than 16 times, and in every draw some expert is named exactly 16 times within some shard; the two experts of a token differ.
All inputs are finite; a program needn't handle non-finite values.
Results may differ from the reference program's by a relative error of at most 0.033.
Values may be sent and summed in bfloat16 or wider, within the bound.
No kernel may reach another device: no remote copies, remote signals or barrier semaphores. Data moves between devices by JAX's collectives and lax.ppermute only.
A program may use at most 64 MiB of HBM per device.

```python
import math
import jax
import jax.numpy as jnp
import numpy as np
from jax import lax

D = 4096
QUERY_HEAD_COUNT = 32
KEY_VALUE_HEADS = 8
HEAD_SIZE = 128
EXPERTS = 8
TOP = 2
H = 8192
S_DEV = 64
SEQUENCE_TOKENS = 1024
CAP = 16
QUART = 4
HB = 128
N_CTX = 16


def key_weight_matrix(key):
    random_seed_key = jax.random.fold_in(key, 11)
    sampled_key_rows = jnp.clip(jax.random.normal(random_seed_key, (SEQUENCE_TOKENS, KEY_VALUE_HEADS * HEAD_SIZE), jnp.float32), -4.0, 4.0)
    return sampled_key_rows


def draw_keys(key, part):
    return key_weight_matrix(key).astype(jnp.bfloat16)


def draw_queries(key, part):
    query_key = jax.random.fold_in(key, 12)
    drawn = jnp.clip(jax.random.normal(query_key, (SEQUENCE_TOKENS, QUERY_HEAD_COUNT * HEAD_SIZE), jnp.float32), -4.0, 4.0)
    return drawn.astype(jnp.bfloat16)


def draw_residual_in(key, part):
    row_key, col_key, value_key = jax.random.split(jax.random.fold_in(key, 31), 3)
    rising = 3.0 ** (jnp.arange(D, dtype=jnp.float32) / (D - 1))
    row_scale = jnp.exp(jax.random.uniform(row_key, (SEQUENCE_TOKENS, 1), jnp.float32, math.log(0.3), math.log(3.0)))
    col_scale = jnp.exp(jax.random.uniform(col_key, (1, D), jnp.float32, math.log(0.3), math.log(3.0))) * rising[None, :]
    drawn = jnp.clip(jax.random.normal(value_key, (SEQUENCE_TOKENS, D), jnp.float32), -3.0, 3.0)
    return (drawn * row_scale * col_scale / 3.0).astype(jnp.bfloat16)


def with_spikes(values, rng, source, target, blocks, factor):
    owner, partner = [(jnp.arange(values.shape[axis_at]) // (values.shape[axis_at] // blocks)).reshape([-1 if axis == axis_at else 1 for axis in range(values.ndim)]) for axis_at in (source, target)]
    chosen = jax.random.permutation(rng, blocks)[partner]
    strong = (owner == chosen) | (owner == (partner + blocks // 2) % blocks)
    return jnp.where(strong, factor * values, values)


def shard_levels(stream_key, shape, cuts, low, largest):
    def one(position, blocks):
        steps = jax.random.uniform(jax.random.fold_in(jax.random.fold_in(stream_key, 6), position), (blocks,), jnp.float32, low / len(cuts), largest / len(cuts))
        return jnp.repeat(jnp.exp(steps), shape[position] // blocks).reshape((-1,) + (1,) * (len(shape) - position - 1))

    factor_of = one(*cuts[0])
    for cut in cuts[1:]:
        factor_of = factor_of * one(*cut)
    return factor_of


def shared_out(stream_key, own, number, rows, number_of, top, limit, slope):
    sequence = jax.random.permutation(stream_key, number_of)
    heavy_load, usual = shares(number_of, rows * top, limit, slope, True), shares(number_of, rows * top, limit, slope, False)
    places = jnp.arange(number_of)

    def named(lengths, offset_by):
        used = int((lengths > 0).sum())
        fixed = max(1, used // 4)
        moved = fixed + (places - fixed + offset_by * (used - fixed)) % max(1, number_of - fixed)
        return jnp.zeros((number_of,), jnp.int32).at[sequence[jnp.where(places < fixed, places, moved)]].set(jnp.asarray(lengths, jnp.int32))

    lengths = jnp.where(number % 4 == 0, named(heavy_load, number // 4), named(usual, number - number // 4 - 1))
    mixed = jax.random.permutation(jax.random.fold_in(own, 3), number_of)
    donor, taker = mixed[0:number_of // 2 * 2:2], mixed[1:number_of // 2 * 2:2]
    room = jnp.minimum(lengths[donor] - 1, limit - lengths[taker]) // 2
    room = jnp.where((donor == sequence[0]) | (taker == sequence[0]) | (lengths[taker] == 0), 0, jnp.maximum(room, 0))
    moved = jax.random.randint(jax.random.fold_in(own, 4), (number_of // 2,), 0, 1 << 20) % (room + 1)
    lengths = lengths.at[donor].add(-moved).at[taker].add(moved)
    labels = jnp.searchsorted(jnp.cumsum(lengths), jnp.arange(rows * top), side="right").astype(jnp.int32)
    table = labels.reshape(top, rows).T
    table = table[jax.random.permutation(jax.random.fold_in(own, 1), rows)]
    offset_by = jax.random.randint(jax.random.fold_in(own, 2), (rows, 1), 0, top)
    return jnp.take_along_axis(table, (jnp.arange(top)[None, :] + offset_by) % top, axis=1)


def shares(number_of, total, limit, skew, full):
    loads = [(1 << 20) // math.isqrt(grade ** skew) + 1 for grade in range(1, number_of + 1)]
    largest = limit if full else min(limit, max(-(-total // number_of), total * loads[0] // sum(loads)))
    least = 1 if total - largest >= number_of - 1 else 0
    given, surplus = [largest] + [least] * (number_of - 1), total - largest - least * (number_of - 1)
    while surplus > 0:
        free = [i for i in range(1, number_of) if given[i] < largest] or [i for i in range(1, number_of) if given[i] < limit]
        whole, left = sum([loads[i] for i in free]), surplus
        for i in free:
            more = min(limit - given[i], max(1, left * loads[i] // whole), surplus)
            given[i] = given[i] + more
            surplus = surplus - more
    return np.array(given)


def scatter_about(stream_key, dims, scale, bound, cuts=(), kind=jnp.bfloat16):
    values = jax.random.normal(stream_key, dims, jnp.float32) * scale
    if len(cuts) > 0:
        values = shard_levels(stream_key, dims, cuts, -0.22, 0.18) * values
    return jnp.clip(values, min=-bound, max=bound).astype(kind)


def gaussian_with(key, shape, deviation, limit, cuts, heavy, kind=jnp.bfloat16):
    values = deviation * jax.random.normal(key, shape, jnp.float32)
    if cuts:
        values = values * shard_levels(key, shape, cuts, -0.22, 0.18)
    return jnp.clip(with_spikes(values, jax.random.fold_in(key, 3), *heavy), -limit, limit).astype(kind)


def setup_inputs(seed: int = 0) -> dict:
    streams_of = jax.random.split(jax.random.key(seed), 12)
    queries = draw_queries(jax.random.fold_in(streams_of[11], 71), 0)
    keys = draw_keys(jax.random.fold_in(streams_of[11], 71), 0)
    values = scatter_about(streams_of[2], (SEQUENCE_TOKENS, KEY_VALUE_HEADS * HEAD_SIZE), 1.0, 6.0, ((0, 16),))
    out_proj = scatter_about(streams_of[3], (QUERY_HEAD_COUNT * HEAD_SIZE, D), (QUERY_HEAD_COUNT * HEAD_SIZE) ** -0.5, 0.09375, ((0, 16), (1, 32)))
    residual_in = draw_residual_in(jax.random.fold_in(streams_of[11], 71), 0)
    norm_gain = jnp.clip(1.0 + 0.18 * jax.random.normal(streams_of[5], (D,), jnp.float32), 0.1, 1.9)
    routes_keys = jax.random.split(jax.random.fold_in(streams_of[6], 1), SEQUENCE_TOKENS // S_DEV)
    routes_turns = jax.random.permutation(jax.random.fold_in(streams_of[6], 3), SEQUENCE_TOKENS // S_DEV)
    routes = jax.vmap(lambda own, number: shared_out(jax.random.fold_in(streams_of[6], 2), own, number, S_DEV, EXPERTS, TOP, CAP, 2))(routes_keys, routes_turns).reshape((SEQUENCE_TOKENS, TOP))
    gate_wts = jnp.clip(0.2 + 0.8 * jax.random.uniform(streams_of[7], (SEQUENCE_TOKENS, TOP), jnp.float32) ** shard_levels(streams_of[7], (SEQUENCE_TOKENS, TOP), ((0, 16),), -0.2, 0.2), 0.2, 1.0)
    w_gate = scatter_about(streams_of[8], (D, EXPERTS * H), D ** -0.5, 0.09375, ((1, 512),))
    w_up = scatter_about(streams_of[9], (D, EXPERTS * H), D ** -0.5, 0.09375, ((1, 512),))
    w_down = gaussian_with(streams_of[10], (EXPERTS * H, D), H ** -0.5, 0.25, ((0, 512),), (0, 1, 512, 6.0))
    return dict(queries=queries, keys=keys, values=values, out_proj=out_proj, residual_in=residual_in, norm_gain=norm_gain, routes=routes, gate_wts=gate_wts, w_gate=w_gate, w_up=w_up, w_down=w_down)


def attention(queries, keys, values):
    seq_len = queries.shape[0]
    query_group_width = QUERY_HEAD_COUNT // KEY_VALUE_HEADS
    score_scale = 1.0 / HEAD_SIZE ** 0.5
    positions = jnp.arange(seq_len, dtype=jnp.int32)
    causal = positions[:, None] >= positions[None, :]

    def one_head(head_num):
        query_head = lax.dynamic_slice_in_dim(queries, head_num * HEAD_SIZE, HEAD_SIZE, 1)
        kv_head = head_num // query_group_width
        key_head = lax.dynamic_slice_in_dim(keys, kv_head * HEAD_SIZE, HEAD_SIZE, 1)
        value_head = lax.dynamic_slice_in_dim(values, kv_head * HEAD_SIZE, HEAD_SIZE, 1)
        scores = jnp.dot(query_head, key_head.T, preferred_element_type=jnp.float32) * score_scale
        scores = jnp.where(causal, scores, -jnp.inf)
        highest = lax.optimization_barrier(jnp.max(scores, axis=1, keepdims=True))
        weights = jnp.exp(scores - highest)
        weight_sum = lax.optimization_barrier(jnp.sum(weights, axis=1, keepdims=True))
        prob_rows = weights.astype(jnp.bfloat16)
        mixed = jnp.dot(prob_rows, value_head, preferred_element_type=jnp.float32) / weight_sum
        return mixed.astype(jnp.bfloat16)
    per_head = lax.map(one_head, jnp.arange(QUERY_HEAD_COUNT, dtype=jnp.int32))
    return jnp.transpose(per_head, (1, 0, 2)).reshape(seq_len, QUERY_HEAD_COUNT * HEAD_SIZE)

def slot_numbers(routes):
    flat_routes = routes.reshape(N_CTX, S_DEV * TOP)
    one_hot = (flat_routes[:, :, None] == jnp.arange(EXPERTS, dtype=jnp.int32)[None, None, :]).astype(jnp.int32)
    earlier = jnp.cumsum(one_hot, axis=1) - one_hot
    return lax.optimization_barrier(jnp.sum(earlier * one_hot, axis=2)).reshape(N_CTX * S_DEV, TOP)

def reference(queries, keys, values, out_proj, residual_in, norm_gain, routes, gate_wts, w_gate, w_up, w_down):
    seq_len = queries.shape[0]
    attn = attention(queries, keys, values)
    resid = residual_in.astype(jnp.float32) + jnp.dot(attn, out_proj, preferred_element_type=jnp.float32)
    residual_out = resid.astype(jnp.bfloat16)
    sq_mean = lax.optimization_barrier(jnp.mean(resid * resid, axis=1, keepdims=True))
    normed = (resid * lax.rsqrt(sq_mean + 1e-05) * norm_gain[None, :]).astype(jnp.bfloat16)
    slot = slot_numbers(routes)
    shard_ids = jnp.arange(seq_len, dtype=jnp.int32) // S_DEV
    buffer = jnp.zeros((EXPERTS, N_CTX, CAP, D), jnp.bfloat16)
    buffer = buffer.at[routes, shard_ids[:, None], slot].set(jnp.broadcast_to(normed[:, None, :], (seq_len, TOP, D)))
    row_total = N_CTX * CAP

    def expert_fn(expert_num):
        rows_in = lax.dynamic_index_in_dim(buffer, expert_num, 0, keepdims=False).reshape(row_total, D)
        gate_cols = lax.dynamic_slice_in_dim(w_gate, expert_num * H, H, 1)
        up_cols = lax.dynamic_slice_in_dim(w_up, expert_num * H, H, 1)
        gate_val = jnp.dot(rows_in, gate_cols, preferred_element_type=jnp.float32)
        up_val = jnp.dot(rows_in, up_cols, preferred_element_type=jnp.float32)
        hidden = (jax.nn.silu(gate_val) * up_val).astype(jnp.bfloat16)

        def quarter_fn(running, quarter_num):

            def block_fn(partial_sum, ctx_num):
                block_num = quarter_num * N_CTX + ctx_num
                hidden_block = lax.dynamic_slice_in_dim(hidden, block_num * HB, HB, 1)
                down_block = lax.dynamic_slice_in_dim(w_down, expert_num * H + block_num * HB, HB, 0)
                piece = jnp.dot(hidden_block, down_block, preferred_element_type=jnp.float32).astype(jnp.bfloat16)
                piece = lax.optimization_barrier(piece)
                return (partial_sum + piece.astype(jnp.float32), None)
            summed, unused = lax.scan(block_fn, jnp.zeros((row_total, D), jnp.float32), jnp.arange(N_CTX, dtype=jnp.int32))
            group = lax.optimization_barrier(summed.astype(jnp.bfloat16))
            return (running + group.astype(jnp.float32), None)
        result, unused = lax.scan(quarter_fn, jnp.zeros((row_total, D), jnp.float32), jnp.arange(QUART, dtype=jnp.int32))
        return result.reshape(N_CTX, CAP, D)
    outputs = lax.map(expert_fn, jnp.arange(EXPERTS, dtype=jnp.int32))
    picked = outputs[routes, shard_ids[:, None], slot]
    expert_out = lax.optimization_barrier(jnp.sum(gate_wts[:, :, None] * picked, axis=1)).astype(jnp.bfloat16)
    return (residual_out, expert_out)
```

```python
import math

import jax
import jax.numpy as jnp
from jax import lax
from jax.sharding import PartitionSpec as P

D = 4096
QUERY_HEAD_COUNT = 32
KEY_VALUE_HEADS = 8
HEAD_SIZE = 128
EXPERTS = 8
TOP = 2
CAP = 16
W_FIRST = 112


def three_terms(value):
    high = lax.reduce_precision(value, 8, 7)
    rest = value - high
    mid = lax.reduce_precision(rest, 8, 7)
    low = rest - mid
    return [part.astype(jnp.bfloat16) for part in (high, mid, low)]


def tie(value, other):
    return value + (other.reshape(-1)[0].astype(jnp.float32) * 0.0).astype(value.dtype)


def slot_index(own_route):
    seg_len = own_route.shape[0]
    experts = jnp.arange(EXPERTS, dtype=jnp.int32)
    named = (own_route[:, :, None] == experts[None, None, :]).astype(jnp.float32)
    rows = jnp.arange(seg_len, dtype=jnp.int32)
    before = (rows[None, :] < rows[:, None]).astype(jnp.bfloat16)
    earlier = jnp.dot(
        before, named.sum(axis=1).astype(jnp.bfloat16), preferred_element_type=jnp.float32
    )
    slot = jnp.sum(named * earlier[:, None, :], axis=2).astype(jnp.int32)
    return own_route * CAP + slot


def per_device(
    queries, keys, values, out_proj, residual_in, norm_gain, routes, gate_wts, w_gate, w_up, w_down
):
    ctx_count = lax.axis_size("ctx")
    exp_count = lax.axis_size("exp")
    ctx_rank = lax.axis_index("ctx")
    exp_rank = lax.axis_index("exp")
    seg_len = queries.shape[0]
    quarters = exp_count // EXPERTS
    rows_dev = CAP // quarters
    pair = [(i, i ^ 1) for i in range(exp_count)]
    chip = [(i, i ^ 2) for i in range(exp_count)]

    near = [w_gate, w_up, w_down]
    far = [lax.ppermute(w, "exp", chip) for w in near]

    kv_first = (exp_rank // (QUERY_HEAD_COUNT // KEY_VALUE_HEADS)) * HEAD_SIZE
    key_part = lax.dynamic_slice_in_dim(keys, kv_first, HEAD_SIZE, 1)
    value_part = lax.dynamic_slice_in_dim(values, kv_first, HEAD_SIZE, 1)
    first = lax.all_gather(
        jnp.concatenate([key_part, value_part, out_proj[:W_FIRST]], axis=0), "ctx", axis=0
    )
    key_all = first[:, :seg_len].reshape(ctx_count * seg_len, HEAD_SIZE)
    value_all = first[:, seg_len : 2 * seg_len].reshape(ctx_count * seg_len, HEAD_SIZE)

    scores = jnp.dot(queries, key_all.T, preferred_element_type=jnp.float32) * (
        1.0 / math.sqrt(HEAD_SIZE)
    )
    query_pos = ctx_rank * seg_len + jnp.arange(seg_len, dtype=jnp.int32)
    key_pos = jnp.arange(ctx_count * seg_len, dtype=jnp.int32)
    visible = query_pos[:, None] >= key_pos[None, :]
    scores = jnp.where(visible, scores, -1e30)
    weights = jnp.where(visible, jnp.exp(scores - jnp.max(scores, axis=1, keepdims=True)), 0.0)
    total = jnp.sum(weights, axis=1, keepdims=True)
    attn = jnp.dot(weights.astype(jnp.bfloat16), value_all, preferred_element_type=jnp.float32)
    attn_local = (attn / total).astype(jnp.bfloat16)

    gain_rows = jnp.stack(three_terms(norm_gain) + [jnp.zeros_like(norm_gain, jnp.bfloat16)] * 5)
    sent = jnp.concatenate([attn_local, gain_rows], axis=0)
    heads = lax.all_to_all(jnp.broadcast_to(sent[None], (exp_count,) + sent.shape), "exp", 0, 0)
    second = lax.all_gather(tie(out_proj[W_FIRST:], attn_local), "ctx", axis=0)
    attn_all = heads[:, :seg_len].transpose(1, 0, 2).reshape(seg_len, D)
    gain_all = heads[:, seg_len : seg_len + 3].astype(jnp.float32).sum(axis=1).reshape(1, D)
    proj = jnp.concatenate([first[:, 2 * seg_len :], second], axis=1).reshape(D, -1)

    residual = residual_in.astype(jnp.float32) + jnp.dot(
        attn_all, proj, preferred_element_type=jnp.float32
    )
    residual_out = residual.astype(jnp.bfloat16)

    own_route = lax.dynamic_slice_in_dim(routes, ctx_rank * seg_len, seg_len, 0)
    place = slot_index(own_route)
    slot_ids = jnp.arange(EXPERTS * CAP, dtype=jnp.int32)
    chosen = (place[:, :, None] == slot_ids[None, None, :]).astype(jnp.float32)
    picked = lax.dot_general(
        chosen.sum(axis=1).astype(jnp.bfloat16),
        residual_out,
        (((0,), (0,)), ((), ())),
        preferred_element_type=jnp.float32,
    ).astype(jnp.bfloat16)
    mine = lax.all_to_all(picked.reshape(exp_count, rows_dev, -1), "exp", 0, 0)
    mine = mine.transpose(1, 0, 2).reshape(rows_dev, D).astype(jnp.float32)
    sq_mean = jnp.mean(mine * mine, axis=1, keepdims=True)
    normed = (mine * lax.rsqrt(sq_mean + 1e-05) * gain_all).astype(jnp.bfloat16)
    rows_all = lax.all_gather(normed, "ctx", axis=0).reshape(ctx_count * rows_dev, D)

    across = [lax.ppermute(w, "exp", pair) for w in near]
    across_far = [lax.ppermute(w, "exp", pair) for w in far]
    out = jnp.zeros((ctx_count * rows_dev, D), jnp.float32)
    for gate_w, up_w, down_w in (near, across, far, across_far):
        gate_val = jnp.dot(rows_all, gate_w, preferred_element_type=jnp.float32)
        up_val = jnp.dot(rows_all, up_w, preferred_element_type=jnp.float32)
        hidden = (jax.nn.silu(gate_val) * up_val).astype(jnp.bfloat16)
        out = out + jnp.dot(hidden, down_w, preferred_element_type=jnp.float32)

    parts = lax.all_to_all(
        out.astype(jnp.bfloat16).reshape(ctx_count, rows_dev, D), "ctx", 0, 0
    )
    summed = parts.astype(jnp.float32).sum(axis=0).astype(jnp.bfloat16)
    back = lax.all_to_all(
        summed.reshape(rows_dev, exp_count, -1).transpose(1, 0, 2), "exp", 0, 0
    ).reshape(EXPERTS * CAP, -1)
    combine = jnp.sum(chosen * gate_wts[:, :, None], axis=1)
    expert_out = jnp.dot(
        combine, back.astype(jnp.float32), precision=lax.Precision.HIGHEST
    ).astype(jnp.bfloat16)
    return (residual_out, expert_out)


def solution(mesh):
    placed = (
        P("ctx", "exp"),
        P("ctx", None),
        P("ctx", None),
        P("ctx", "exp"),
        P("ctx", "exp"),
        P("exp"),
        P(),
        P("ctx", None),
        P(None, ("exp", "ctx")),
        P(None, ("exp", "ctx")),
        P(("exp", "ctx"), None),
    )
    return jax.shard_map(
        per_device,
        mesh=mesh,
        in_specs=placed,
        out_specs=(P("ctx", "exp"), P("ctx", "exp")),
        check_vma=False,
    )
```

```python
import math

import jax
import jax.numpy as jnp
from jax import lax
from jax.experimental import pallas as pl
from jax.experimental.pallas import tpu as pltpu
from jax.sharding import PartitionSpec as P

D = 4096
QUERY_HEAD_COUNT = 32
KEY_VALUE_HEADS = 8
HEAD_SIZE = 128
EXPERTS = 8
TOP = 2
CAP = 16
SEG = 64
SHARDS = 16
W_FIRST = 112
EXTRA = 16

VMEM = pl.BlockSpec(memory_space=pltpu.VMEM)
SMEM = pl.BlockSpec(memory_space=pltpu.SMEM)
ANY = pl.BlockSpec(memory_space=pl.ANY)
ATTENTION_ROOM = 16 * 1024 * 1024
ROOM = 63 * 1024 * 1024 - 512 * 1024
F32 = jnp.float32
BF16 = jnp.bfloat16


def three_terms(value):
    high = value.astype(BF16)
    rest = value - high.astype(F32)
    mid = rest.astype(BF16)
    return [high, mid, (rest - mid.astype(F32)).astype(BF16)]


def slot_places(routes):
    seg_len = routes.shape[1]
    experts = jnp.arange(EXPERTS, dtype=jnp.int32)
    named = (routes[:, :, :, None] == experts).astype(F32)
    rows = jnp.arange(seg_len, dtype=jnp.int32)
    before = (rows[None, :] < rows[:, None]).astype(BF16)
    earlier = jnp.einsum(
        "ts,cse->cte", before, named.sum(axis=2).astype(BF16), preferred_element_type=F32
    )
    slot = jnp.sum(named * earlier[:, :, None, :], axis=3).astype(jnp.int32)
    return routes * CAP + slot


def pack_kernel(
    head_ref, gate_ref, up_ref, down_ref, key_ref, value_ref, proj_ref,
    out_ref, first_ref, gate_v, up_v, down_v, packed_v, sems,
):
    column = pl.ds(pl.multiple_of(head_ref[0] * HEAD_SIZE, HEAD_SIZE), HEAD_SIZE)
    copies = [
        pltpu.make_async_copy(src, dst, sems.at[i])
        for i, (src, dst) in enumerate(
            (
                (down_ref, down_v),
                (gate_ref, gate_v),
                (up_ref, up_v),
                (key_ref.at[:, column], first_ref.at[pl.ds(0, SEG)]),
                (value_ref.at[:, column], first_ref.at[pl.ds(SEG, SEG)]),
                (proj_ref.at[pl.ds(0, W_FIRST)], first_ref.at[pl.ds(2 * SEG, W_FIRST)]),
            )
        )
    ]
    for copy in copies:
        copy.start()
    outs = [
        pltpu.make_async_copy(src, out_ref.at[pl.ds(i * D, D)], sems.at[6 + i])
        for i, src in enumerate((gate_v, up_v, packed_v))
    ]
    copies[0].wait()
    for b in range(D // 128):
        packed_v[b * 128 : (b + 1) * 128] = down_v[:, b * 128 : (b + 1) * 128]
    outs[2].start()
    copies[1].wait()
    outs[0].start()
    copies[2].wait()
    outs[1].start()
    for copy in copies[3:] + outs:
        copy.wait()


def pack(head, w_gate, w_up, w_down, keys, values, out_proj):
    return pl.pallas_call(
        pack_kernel,
        out_shape=[
            jax.ShapeDtypeStruct((3 * D, 128), BF16),
            jax.ShapeDtypeStruct((2 * SEG + W_FIRST, HEAD_SIZE), BF16),
        ],
        in_specs=[SMEM] + [ANY] * 6,
        out_specs=[ANY, VMEM],
        scratch_shapes=[
            pltpu.VMEM((D, 128), BF16),
            pltpu.VMEM((D, 128), BF16),
            pltpu.VMEM((128, D), BF16),
            pltpu.VMEM((D, 128), BF16),
            pltpu.SemaphoreType.DMA((9,)),
        ],
        compiler_params=pltpu.CompilerParams(vmem_limit_bytes=ROOM),
    )(head, w_gate, w_up, w_down, keys, values, out_proj)


def attention_kernel(
    ctx_ref, query_ref, first_ref, gain_ref, gate_ref, proj_ref, out_ref, second_ref
):
    second_ref[: proj_ref.shape[0] - W_FIRST] = proj_ref[W_FIRST:]
    second_ref[proj_ref.shape[0] - W_FIRST :] = gate_ref[...]
    count = SHARDS * SEG
    key_all = first_ref[:, :SEG].reshape(count, HEAD_SIZE)
    value_all = first_ref[:, SEG : 2 * SEG].reshape(count, HEAD_SIZE)
    scores = lax.dot_general(
        query_ref[...], key_all, (((1,), (1,)), ((), ())), preferred_element_type=F32
    ) * (1.0 / math.sqrt(HEAD_SIZE))
    row = lax.broadcasted_iota(jnp.int32, scores.shape, 0) + ctx_ref[0] * SEG
    visible = row >= lax.broadcasted_iota(jnp.int32, scores.shape, 1)
    scores = jnp.where(visible, scores, -1e30)
    weights = jnp.where(visible, jnp.exp(scores - jnp.max(scores, axis=1, keepdims=True)), 0.0)
    total = jnp.sum(weights, axis=1, keepdims=True)
    attn = jnp.dot(weights.astype(BF16), value_all, preferred_element_type=F32)
    gains = three_terms(jnp.broadcast_to(gain_ref[...], (EXTRA, HEAD_SIZE)))
    line = lax.broadcasted_iota(jnp.int32, (EXTRA, HEAD_SIZE), 0)
    gain_rows = jnp.zeros((EXTRA, HEAD_SIZE), F32)
    for k in range(3):
        gain_rows = jnp.where(line == k, gains[k].astype(F32), gain_rows)
    sent = jnp.concatenate([(attn / total).astype(BF16), gain_rows.astype(BF16)], axis=0)
    out_ref[...] = jnp.broadcast_to(sent[None], out_ref.shape)


def attention(ctx_rank, queries, first, gain, gate_rows, out_proj):
    return pl.pallas_call(
        attention_kernel,
        out_shape=[
            jax.ShapeDtypeStruct((QUERY_HEAD_COUNT, SEG + EXTRA, HEAD_SIZE), BF16),
            jax.ShapeDtypeStruct((out_proj.shape[0] - W_FIRST + EXTRA, HEAD_SIZE), BF16),
        ],
        in_specs=[SMEM] + [VMEM] * 5,
        out_specs=[VMEM, VMEM],
        compiler_params=pltpu.CompilerParams(vmem_limit_bytes=ATTENTION_ROOM),
    )(ctx_rank, queries, first, gain, gate_rows, out_proj)


def project_kernel(
    heads_ref, first_ref, second_ref, residual_ref, chosen_ref, near_ref, far_ref,
    out_ref, picked_ref, gain_ref, near_out, far_out, attn_v, proj_v,
):
    del near_ref, far_ref, near_out, far_out
    for h in range(QUERY_HEAD_COUNT):
        attn_v[:, h * 128 : (h + 1) * 128] = heads_ref[h, :SEG]
        gain_ref[:, h * 128 : (h + 1) * 128] = jnp.sum(
            heads_ref[h, SEG:].astype(F32), axis=0, keepdims=True
        )
    for c in range(SHARDS):
        proj_v[c * 256 : c * 256 + W_FIRST] = first_ref[c, 2 * SEG : 2 * SEG + W_FIRST]
        proj_v[c * 256 + W_FIRST : (c + 1) * 256] = second_ref[c, : 256 - W_FIRST]
    residual = residual_ref[...].astype(F32) + jnp.dot(
        attn_v[...], proj_v[...], preferred_element_type=F32
    )
    rounded = residual.astype(BF16)
    out_ref[...] = rounded
    picked_ref[...] = jnp.dot(
        chosen_ref[...], rounded, preferred_element_type=F32
    ).astype(BF16)


def project(heads, first, second, residual_in, chosen, near, far):
    return pl.pallas_call(
        project_kernel,
        out_shape=[
            jax.ShapeDtypeStruct((SEG, 128), BF16),
            jax.ShapeDtypeStruct((EXPERTS * CAP, 128), BF16),
            jax.ShapeDtypeStruct((1, D), F32),
            jax.ShapeDtypeStruct(near.shape, near.dtype),
            jax.ShapeDtypeStruct(far.shape, far.dtype),
        ],
        in_specs=[VMEM] * 5 + [ANY] * 2,
        out_specs=[VMEM] * 3 + [ANY] * 2,
        scratch_shapes=[pltpu.VMEM((SEG, D), BF16), pltpu.VMEM((D, 128), BF16)],
        input_output_aliases={5: 3, 6: 4},
        compiler_params=pltpu.CompilerParams(vmem_limit_bytes=ROOM),
    )(heads, first, second, residual_in, chosen, near, far)


def experts_kernel(x_ref, *refs):
    weights, (out_ref, held_v, hidden_v, sems) = refs[:4], refs[4:]
    copies = []
    for part in range(2):
        for i in range(4):
            rows = pl.ds(part * 2 * D, 2 * D if part == 0 else D)
            copies.append(
                pltpu.make_async_copy(weights[i].at[rows], held_v.at[i, rows], sems.at[i, part])
            )
    for copy in copies:
        copy.start()
    x = jnp.concatenate([x_ref[c].astype(F32) for c in range(SHARDS)], axis=0).astype(BF16)
    for i in range(4):
        copies[i].wait()
        both = jnp.dot(
            x,
            jnp.concatenate([held_v[i, :D], held_v[i, D : 2 * D]], axis=1),
            preferred_element_type=F32,
        )
        gate_val, up_val = both[:, :128], both[:, 128:]
        hidden_v[:, i * 128 : (i + 1) * 128] = (
            gate_val / (1.0 + jnp.exp(-gate_val)) * up_val
        ).astype(BF16)
    for i in range(4):
        copies[4 + i].wait()
    hidden = hidden_v[...]
    for b in range(0, D // 128, 2):
        start = 2 * D + b * 128
        down = jnp.concatenate(
            [
                jnp.concatenate(
                    [held_v[i, start : start + 128], held_v[i, start + 128 : start + 256]], axis=1
                )
                for i in range(4)
            ],
            axis=0,
        )
        part = jnp.dot(hidden, down, preferred_element_type=F32).astype(BF16)
        out_ref[b] = part[:, :128]
        out_ref[b + 1] = part[:, 128:]


def run_experts(rows_all, weights):
    rows = rows_all.shape[0] * rows_all.shape[1]
    return pl.pallas_call(
        experts_kernel,
        out_shape=jax.ShapeDtypeStruct((D // 128, rows, 128), BF16),
        in_specs=[VMEM] + [ANY] * 4,
        out_specs=VMEM,
        scratch_shapes=[
            pltpu.VMEM((4, 3 * D, 128), BF16),
            pltpu.VMEM((rows, 512), BF16),
            pltpu.SemaphoreType.DMA((4, 2)),
        ],
        compiler_params=pltpu.CompilerParams(vmem_limit_bytes=ROOM),
        cost_estimate=pl.CostEstimate(
            flops=2 * rows * 512 * D * 3, bytes_accessed=12 * 128 * D * 2, transcendentals=0
        ),
    )(rows_all, *weights)


def weigh_kernel(parts_ref, combine_ref, out_ref):
    for g in range(SHARDS // 4):
        rows = parts_ref[:, g * 16 : (g + 1) * 16].reshape(QUERY_HEAD_COUNT * 16, 128)
        total = jnp.dot(combine_ref[g], rows, preferred_element_type=F32)
        out_ref[g * 4 : (g + 1) * 4] = total.astype(BF16).reshape(4, SEG, 128)


def weigh(parts, combine):
    return pl.pallas_call(
        weigh_kernel,
        out_shape=jax.ShapeDtypeStruct((SHARDS, SEG, 128), BF16),
        in_specs=[VMEM] * 2,
        out_specs=VMEM,
        compiler_params=pltpu.CompilerParams(vmem_limit_bytes=16 * 1024 * 1024),
    )(parts, combine)


def per_device(
    queries, keys, values, out_proj, residual_in, norm_gain, routes, gate_wts, w_gate, w_up, w_down
):
    ctx_count = lax.axis_size("ctx")
    exp_count = lax.axis_size("exp")
    ctx_rank = lax.axis_index("ctx")
    exp_rank = lax.axis_index("exp")
    rows_dev = CAP // (exp_count // EXPERTS)
    pair = [(i, i ^ 1) for i in range(exp_count)]
    chip = [(i, i ^ 2) for i in range(exp_count)]

    head = (exp_rank // (QUERY_HEAD_COUNT // KEY_VALUE_HEADS)).astype(jnp.int32).reshape(1)
    near, sent = pack(head, w_gate, w_up, w_down, keys, values, out_proj)
    far = lax.ppermute(near, "exp", chip)

    first = lax.all_gather(sent, "ctx", axis=0)
    gate_row = gate_wts.T.reshape(1, TOP * SEG).astype(BF16)
    spread, rest = attention(
        ctx_rank.astype(jnp.int32).reshape(1),
        queries,
        first,
        norm_gain.reshape(1, -1),
        jnp.concatenate([gate_row, jnp.zeros((EXTRA - 1, TOP * SEG), BF16)], axis=0),
        out_proj,
    )
    heads = lax.all_to_all(spread, "exp", 0, 0)
    second = lax.all_gather(rest, "ctx", axis=0)
    gate_all = second[:, -EXTRA].reshape(ctx_count, TOP, SEG)

    place = slot_places(routes.reshape(ctx_count, SEG, TOP))
    own_place = lax.dynamic_index_in_dim(place, ctx_rank, 0, keepdims=False)
    slot_ids = jnp.arange(EXPERTS * CAP, dtype=jnp.int32)
    chosen = (own_place.T[:, None, :] == slot_ids[None, :, None]).astype(F32).sum(axis=0)
    shard = jnp.arange(ctx_count, dtype=jnp.int32)[:, None, None] % 4
    column = (place // rows_dev) * 16 + shard * rows_dev + place % rows_dev
    columns = jnp.arange(exp_count * 16, dtype=jnp.int32)
    combine = sum(
        jnp.where(column[:, :, k, None] == columns, gate_all[:, k, :, None], jnp.zeros((), BF16))
        for k in range(TOP)
    ).reshape(ctx_count // 4, 4 * SEG, exp_count * 16)

    residual_out, picked, gain_all, near, far = project(
        heads, first, second, residual_in, chosen.astype(BF16), near, far
    )
    across = lax.ppermute(near, "exp", pair)
    across_far = lax.ppermute(far, "exp", pair)

    mine = lax.all_to_all(picked.reshape(exp_count, rows_dev, -1), "exp", 0, 0)
    mine = mine.transpose(1, 0, 2).reshape(rows_dev, D).astype(F32)
    sq_mean = jnp.mean(mine * mine, axis=1, keepdims=True)
    normed = (mine * lax.rsqrt(sq_mean + 1e-05) * gain_all).astype(BF16)
    rows_all = lax.all_gather(normed, "ctx", axis=0)

    out = run_experts(rows_all, [near, across, far, across_far])

    parts = lax.all_to_all(out, "exp", 0, 0)
    pieces = lax.all_to_all(weigh(parts, combine), "ctx", 0, 0)
    expert_out = pieces.astype(F32).sum(axis=0).astype(BF16)
    return (residual_out, expert_out)


def solution(mesh):
    placed = (
        P("ctx", "exp"),
        P("ctx", None),
        P("ctx", None),
        P("ctx", "exp"),
        P("ctx", "exp"),
        P("exp"),
        P(),
        P("ctx", None),
        P(None, ("exp", "ctx")),
        P(None, ("exp", "ctx")),
        P(("exp", "ctx"), None),
    )
    return jax.shard_map(
        per_device,
        mesh=mesh,
        in_specs=placed,
        out_specs=(P("ctx", "exp"), P("ctx", "exp")),
        check_vma=False,
    )
```

```python
import math

import jax
import jax.numpy as jnp
from jax import lax
from jax.experimental import pallas as pl
from jax.experimental.pallas import tpu as pltpu
from jax.sharding import PartitionSpec as P

D = 4096
QUERY_HEAD_COUNT = 32
KEY_VALUE_HEADS = 8
HEAD_SIZE = 128
EXPERTS = 8
TOP = 2
CAP = 16
SEG = 64
SHARDS = 16
W_FIRST = 112
EXTRA = 16

VMEM = pl.BlockSpec(memory_space=pltpu.VMEM)
SMEM = pl.BlockSpec(memory_space=pltpu.SMEM)
ANY = pl.BlockSpec(memory_space=pl.ANY)
PACK_ROOM = 60 * 1024 * 1024
ATTENTION_ROOM = 16 * 1024 * 1024
ROOM = 63 * 1024 * 1024 - 512 * 1024
F32 = jnp.float32
BF16 = jnp.bfloat16


def three_terms(value):
    high = value.astype(BF16)
    rest = value - high.astype(F32)
    mid = rest.astype(BF16)
    return [high, mid, (rest - mid.astype(F32)).astype(BF16)]


def slot_places(routes):
    seg_len = routes.shape[1]
    experts = jnp.arange(EXPERTS, dtype=jnp.int32)
    named = (routes[:, :, :, None] == experts).astype(F32)
    rows = jnp.arange(seg_len, dtype=jnp.int32)
    before = (rows[None, :] < rows[:, None]).astype(BF16)
    earlier = jnp.einsum(
        "ts,cse->cte", before, named.sum(axis=2).astype(BF16), preferred_element_type=F32
    )
    slot = jnp.sum(named * earlier[:, :, None, :], axis=3).astype(jnp.int32)
    return routes * CAP + slot


def pack_kernel(
    head_ref, gate_ref, up_ref, down_ref, key_ref, value_ref, proj_ref,
    out_ref, first_ref, down_v, sems,
):
    column = pl.ds(pl.multiple_of(head_ref[0] * HEAD_SIZE, HEAD_SIZE), HEAD_SIZE)
    copies = [
        pltpu.make_async_copy(src, dst, sems.at[i])
        for i, (src, dst) in enumerate(
            (
                (down_ref, down_v),
                (gate_ref, out_ref.at[pl.ds(0, D)]),
                (up_ref, out_ref.at[pl.ds(D, D)]),
                (key_ref.at[:, column], first_ref.at[pl.ds(0, SEG)]),
                (value_ref.at[:, column], first_ref.at[pl.ds(SEG, SEG)]),
                (proj_ref.at[pl.ds(0, W_FIRST)], first_ref.at[pl.ds(2 * SEG, W_FIRST)]),
            )
        )
    ]
    for copy in copies:
        copy.start()
    copies[0].wait()
    for b in range(D // 128):
        out_ref[2 * D + b * 128 : 2 * D + (b + 1) * 128] = down_v[:, b * 128 : (b + 1) * 128]
    for copy in copies[1:]:
        copy.wait()


def pack(head, w_gate, w_up, w_down, keys, values, out_proj):
    return pl.pallas_call(
        pack_kernel,
        out_shape=[
            jax.ShapeDtypeStruct((3 * D, 128), BF16),
            jax.ShapeDtypeStruct((2 * SEG + W_FIRST, HEAD_SIZE), BF16),
        ],
        in_specs=[SMEM] + [ANY] * 6,
        out_specs=[VMEM, VMEM],
        scratch_shapes=[pltpu.VMEM((128, D), BF16), pltpu.SemaphoreType.DMA((6,))],
        compiler_params=pltpu.CompilerParams(vmem_limit_bytes=PACK_ROOM),
    )(head, w_gate, w_up, w_down, keys, values, out_proj)


def attention_kernel(
    ctx_ref, query_ref, first_ref, gain_ref, gate_ref, proj_ref, out_ref, second_ref
):
    second_ref[: proj_ref.shape[0] - W_FIRST] = proj_ref[W_FIRST:]
    wts = jnp.concatenate([gate_ref[...], jnp.zeros((TOP, HEAD_SIZE - SEG), F32)], axis=1)
    line = lax.broadcasted_iota(jnp.int32, (EXTRA, HEAD_SIZE), 0)
    second_ref[proj_ref.shape[0] - W_FIRST :] = jnp.where(
        line == 0, wts[0:1], jnp.where(line == 1, wts[1:2], 0.0)
    ).astype(BF16)
    count = SHARDS * SEG
    key_all = first_ref[:, :SEG].reshape(count, HEAD_SIZE)
    value_all = first_ref[:, SEG : 2 * SEG].reshape(count, HEAD_SIZE)
    scores = lax.dot_general(
        query_ref[...], key_all, (((1,), (1,)), ((), ())), preferred_element_type=F32
    ) * (1.0 / math.sqrt(HEAD_SIZE))
    row = lax.broadcasted_iota(jnp.int32, scores.shape, 0) + ctx_ref[0] * SEG
    visible = row >= lax.broadcasted_iota(jnp.int32, scores.shape, 1)
    scores = jnp.where(visible, scores, -1e30)
    weights = jnp.where(visible, jnp.exp(scores - jnp.max(scores, axis=1, keepdims=True)), 0.0)
    total = jnp.sum(weights, axis=1, keepdims=True)
    attn = jnp.dot(weights.astype(BF16), value_all, preferred_element_type=F32)
    gains = three_terms(jnp.broadcast_to(gain_ref[...], (EXTRA, HEAD_SIZE)))
    gain_rows = jnp.zeros((EXTRA, HEAD_SIZE), F32)
    for k in range(3):
        gain_rows = jnp.where(line == k, gains[k].astype(F32), gain_rows)
    sent = jnp.concatenate([(attn / total).astype(BF16), gain_rows.astype(BF16)], axis=0)
    out_ref[...] = jnp.broadcast_to(sent[None], out_ref.shape)


def attention(ctx_rank, queries, first, gain, wts, out_proj):
    return pl.pallas_call(
        attention_kernel,
        out_shape=[
            jax.ShapeDtypeStruct((QUERY_HEAD_COUNT, SEG + EXTRA, HEAD_SIZE), BF16),
            jax.ShapeDtypeStruct((out_proj.shape[0] - W_FIRST + EXTRA, HEAD_SIZE), BF16),
        ],
        in_specs=[SMEM] + [VMEM] * 5,
        out_specs=[VMEM, VMEM],
        compiler_params=pltpu.CompilerParams(vmem_limit_bytes=ATTENTION_ROOM),
    )(ctx_rank, queries, first, gain, wts, out_proj)


def project_kernel(
    ctx_ref, heads_ref, first_ref, second_ref, residual_ref, place_ref,
    out_ref, picked_ref, gain_ref, attn_v, proj_v,
):
    for h in range(QUERY_HEAD_COUNT):
        attn_v[:, h * 128 : (h + 1) * 128] = heads_ref[h, :SEG]
        gain_ref[:, h * 128 : (h + 1) * 128] = jnp.sum(
            heads_ref[h, SEG:].astype(F32), axis=0, keepdims=True
        )
    for c in range(SHARDS):
        proj_v[c * 256 : c * 256 + W_FIRST] = first_ref[c, 2 * SEG : 2 * SEG + W_FIRST]
        proj_v[c * 256 + W_FIRST : (c + 1) * 256] = second_ref[c, : 256 - W_FIRST]
    residual = residual_ref[...].astype(F32) + jnp.dot(
        attn_v[...], proj_v[...], preferred_element_type=F32
    )
    rounded = residual.astype(BF16)
    out_ref[...] = rounded
    line = lax.broadcasted_iota(jnp.int32, (EXPERTS * CAP, SEG), 0)
    place = place_ref[ctx_ref[0]]
    chosen = jnp.where((line == place[0:1]) | (line == place[1:2]), 1.0, 0.0)
    picked_ref[...] = jnp.dot(chosen.astype(BF16), rounded, preferred_element_type=F32).astype(BF16)


def project(ctx_rank, heads, first, second, residual_in, place):
    return pl.pallas_call(
        project_kernel,
        out_shape=[
            jax.ShapeDtypeStruct((SEG, 128), BF16),
            jax.ShapeDtypeStruct((EXPERTS * CAP, 128), BF16),
            jax.ShapeDtypeStruct((1, D), F32),
        ],
        in_specs=[SMEM] + [VMEM] * 5,
        out_specs=[VMEM] * 3,
        scratch_shapes=[pltpu.VMEM((SEG, D), BF16), pltpu.VMEM((D, 128), BF16)],
        compiler_params=pltpu.CompilerParams(vmem_limit_bytes=ATTENTION_ROOM),
    )(ctx_rank, heads, first, second, residual_in, place)


def after_kernel(near_ref, far_ref, other_ref, near_out, far_out):
    del near_ref, far_ref, other_ref, near_out, far_out


def after(near, far, other):
    return pl.pallas_call(
        after_kernel,
        out_shape=[jax.ShapeDtypeStruct(v.shape, v.dtype) for v in (near, far)],
        in_specs=[ANY, ANY, ANY],
        out_specs=[ANY, ANY],
        input_output_aliases={0: 0, 1: 1},
        compiler_params=pltpu.CompilerParams(vmem_limit_bytes=ROOM),
    )(near, far, other)


def experts_kernel(x_ref, *refs):
    weights, (out_ref, held_v, hidden_v, sems) = refs[:4], refs[4:]
    copies = []
    for part in range(2):
        for i in range(4):
            rows = pl.ds(part * 2 * D, 2 * D if part == 0 else D)
            copies.append(
                pltpu.make_async_copy(weights[i].at[rows], held_v.at[i, rows], sems.at[i, part])
            )
    for copy in copies:
        copy.start()
    x = x_ref[...]
    for i in range(4):
        copies[i].wait()
        both = jnp.dot(
            x,
            jnp.concatenate([held_v[i, :D], held_v[i, D : 2 * D]], axis=1),
            preferred_element_type=F32,
        )
        gate_val, up_val = both[:, :128], both[:, 128:]
        hidden_v[:, i * 128 : (i + 1) * 128] = (
            gate_val / (1.0 + jnp.exp(-gate_val)) * up_val
        ).astype(BF16)
    for i in range(4):
        copies[4 + i].wait()
    hidden = hidden_v[...]
    for b in range(0, D // 128, 2):
        start = 2 * D + b * 128
        down = jnp.concatenate(
            [
                jnp.concatenate(
                    [held_v[i, start : start + 128], held_v[i, start + 128 : start + 256]], axis=1
                )
                for i in range(4)
            ],
            axis=0,
        )
        part = jnp.dot(hidden, down, preferred_element_type=F32).astype(BF16)
        out_ref[b] = part[:, :128]
        out_ref[b + 1] = part[:, 128:]


def run_experts(rows_all, weights):
    rows = rows_all.shape[0]
    return pl.pallas_call(
        experts_kernel,
        out_shape=jax.ShapeDtypeStruct((D // 128, rows, 128), BF16),
        in_specs=[VMEM] + [ANY] * 4,
        out_specs=VMEM,
        scratch_shapes=[
            pltpu.VMEM((4, 3 * D, 128), BF16),
            pltpu.VMEM((rows, 512), BF16),
            pltpu.SemaphoreType.DMA((4, 2)),
        ],
        compiler_params=pltpu.CompilerParams(vmem_limit_bytes=ROOM),
        cost_estimate=pl.CostEstimate(
            flops=2 * rows * 512 * D * 3, bytes_accessed=12 * 128 * D * 2, transcendentals=0
        ),
    )(rows_all, *weights)


def weigh_kernel(parts_ref, combine_ref, out_ref):
    for g in range(SHARDS // 4):
        rows = parts_ref[:, g * 16 : (g + 1) * 16].reshape(QUERY_HEAD_COUNT * 16, 128)
        total = jnp.dot(combine_ref[g], rows, preferred_element_type=F32)
        out_ref[g * 4 : (g + 1) * 4] = total.astype(BF16).reshape(4, SEG, 128)


def weigh(parts, combine):
    return pl.pallas_call(
        weigh_kernel,
        out_shape=jax.ShapeDtypeStruct((SHARDS, SEG, 128), BF16),
        in_specs=[VMEM] * 2,
        out_specs=VMEM,
        compiler_params=pltpu.CompilerParams(vmem_limit_bytes=16 * 1024 * 1024),
    )(parts, combine)


def per_device(
    queries, keys, values, out_proj, residual_in, norm_gain, routes, gate_wts, w_gate, w_up, w_down
):
    ctx_count = lax.axis_size("ctx")
    exp_count = lax.axis_size("exp")
    ctx_rank = lax.axis_index("ctx")
    exp_rank = lax.axis_index("exp")
    rows_dev = CAP // (exp_count // EXPERTS)
    pair = [(i, i ^ 1) for i in range(exp_count)]
    chip = [(i, i ^ 2) for i in range(exp_count)]

    ctx = ctx_rank.astype(jnp.int32).reshape(1)

    head = (exp_rank // (QUERY_HEAD_COUNT // KEY_VALUE_HEADS)).astype(jnp.int32).reshape(1)
    near, sent = pack(head, w_gate, w_up, w_down, keys, values, out_proj)
    far = lax.ppermute(near, "exp", chip)

    first = lax.all_gather(sent, "ctx", axis=0)
    spread, rest = attention(
        ctx,
        queries,
        first,
        norm_gain.reshape(1, -1),
        gate_wts.T,
        out_proj,
    )
    heads = lax.all_to_all(spread, "exp", 0, 0)
    second = lax.all_gather(rest, "ctx", axis=0)
    gate_all = second[:, -EXTRA : TOP - EXTRA, :SEG]

    place = slot_places(routes.reshape(ctx_count, SEG, TOP))
    shard = jnp.arange(ctx_count, dtype=jnp.int32)[:, None, None] % 4
    column = (place // rows_dev) * 16 + shard * rows_dev + place % rows_dev
    columns = jnp.arange(exp_count * 16, dtype=jnp.int32)
    combine = sum(
        jnp.where(column[:, :, k, None] == columns, gate_all[:, k, :, None], jnp.zeros((), BF16))
        for k in range(TOP)
    ).reshape(ctx_count // 4, 4 * SEG, exp_count * 16)

    residual_out, picked, gain_all = project(
        ctx, heads, first, second, residual_in, place.transpose(0, 2, 1)
    )
    near, far = after(near, far, residual_out)
    across = lax.ppermute(near, "exp", pair)
    across_far = lax.ppermute(far, "exp", pair)

    mine = lax.all_to_all(picked.reshape(exp_count, rows_dev, -1), "exp", 0, 0)
    mine = mine.transpose(1, 0, 2).reshape(rows_dev, D).astype(F32)
    sq_mean = jnp.mean(mine * mine, axis=1, keepdims=True)
    normed = (mine * lax.rsqrt(sq_mean + 1e-05) * gain_all).astype(BF16)
    rows_all = lax.all_gather(normed, "ctx", axis=0).reshape(ctx_count * rows_dev, D)

    out = run_experts(rows_all, [near, across, far, across_far])

    parts = lax.all_to_all(out, "exp", 0, 0)
    pieces = lax.all_to_all(weigh(parts, combine), "ctx", 0, 0)
    expert_out = pieces.astype(F32).sum(axis=0).astype(BF16)
    return (residual_out, expert_out)


def solution(mesh):
    placed = (
        P("ctx", "exp"),
        P("ctx", None),
        P("ctx", None),
        P("ctx", "exp"),
        P("ctx", "exp"),
        P("exp"),
        P(),
        P("ctx", None),
        P(None, ("exp", "ctx")),
        P(None, ("exp", "ctx")),
        P(("exp", "ctx"), None),
    )
    return jax.shard_map(
        per_device,
        mesh=mesh,
        in_specs=placed,
        out_specs=(P("ctx", "exp"), P("ctx", "exp")),
        check_vma=False,
    )
```

```python
import math

import jax
import jax.numpy as jnp
from jax import lax
from jax.experimental import pallas as pl
from jax.experimental.pallas import tpu as pltpu
from jax.sharding import PartitionSpec as P

D = 4096
QUERY_HEAD_COUNT = 32
KEY_VALUE_HEADS = 8
HEAD_SIZE = 128
EXPERTS = 8
TOP = 2
CAP = 16
SEG = 64
SHARDS = 16
W_FIRST = 64
EXTRA = 16

VMEM = pl.BlockSpec(memory_space=pltpu.VMEM)
SMEM = pl.BlockSpec(memory_space=pltpu.SMEM)
ANY = pl.BlockSpec(memory_space=pl.ANY)
PACK_ROOM = 60 * 1024 * 1024
ATTENTION_ROOM = 16 * 1024 * 1024
ROOM = 63 * 1024 * 1024 - 512 * 1024
F32 = jnp.float32
BF16 = jnp.bfloat16


def three_terms(value):
    high = value.astype(BF16)
    rest = value - high.astype(F32)
    mid = rest.astype(BF16)
    return [high, mid, (rest - mid.astype(F32)).astype(BF16)]


def slot_places(routes):
    seg_len = routes.shape[1]
    experts = jnp.arange(EXPERTS, dtype=jnp.int32)
    named = (routes[:, :, :, None] == experts).astype(F32)
    rows = jnp.arange(seg_len, dtype=jnp.int32)
    before = (rows[None, :] < rows[:, None]).astype(BF16)
    earlier = jnp.einsum(
        "ts,cse->cte", before, named.sum(axis=2).astype(BF16), preferred_element_type=F32
    )
    slot = jnp.sum(named * earlier[:, :, None, :], axis=3).astype(jnp.int32)
    return routes * CAP + slot


def pack_kernel(
    head_ref, gate_ref, up_ref, down_ref, key_ref, value_ref, proj_ref,
    out_ref, first_ref, down_v, sems,
):
    column = pl.ds(pl.multiple_of(head_ref[0] * HEAD_SIZE, HEAD_SIZE), HEAD_SIZE)
    copies = [
        pltpu.make_async_copy(src, dst, sems.at[i])
        for i, (src, dst) in enumerate(
            (
                (down_ref, down_v),
                (gate_ref, out_ref.at[pl.ds(0, D)]),
                (up_ref, out_ref.at[pl.ds(D, D)]),
                (key_ref.at[:, column], first_ref.at[pl.ds(0, SEG)]),
                (value_ref.at[:, column], first_ref.at[pl.ds(SEG, SEG)]),
                (proj_ref.at[pl.ds(0, W_FIRST)], first_ref.at[pl.ds(2 * SEG, W_FIRST)]),
            )
        )
    ]
    for copy in copies:
        copy.start()
    copies[0].wait()
    for b in range(D // 128):
        out_ref[2 * D + b * 128 : 2 * D + (b + 1) * 128] = down_v[:, b * 128 : (b + 1) * 128]
    for copy in copies[1:]:
        copy.wait()


def pack(head, w_gate, w_up, w_down, keys, values, out_proj):
    return pl.pallas_call(
        pack_kernel,
        out_shape=[
            jax.ShapeDtypeStruct((3 * D, 128), BF16),
            jax.ShapeDtypeStruct((2 * SEG + W_FIRST, HEAD_SIZE), BF16),
        ],
        in_specs=[SMEM] + [ANY] * 6,
        out_specs=[VMEM, VMEM],
        scratch_shapes=[pltpu.VMEM((128, D), BF16), pltpu.SemaphoreType.DMA((6,))],
        compiler_params=pltpu.CompilerParams(vmem_limit_bytes=PACK_ROOM),
    )(head, w_gate, w_up, w_down, keys, values, out_proj)


def attention_kernel(
    ctx_ref, query_ref, first_ref, gain_ref, gate_ref, proj_ref, out_ref, second_ref
):
    second_ref[: proj_ref.shape[0] - W_FIRST] = proj_ref[W_FIRST:]
    wts = jnp.concatenate([gate_ref[...], jnp.zeros((TOP, HEAD_SIZE - SEG), F32)], axis=1)
    line = lax.broadcasted_iota(jnp.int32, (EXTRA, HEAD_SIZE), 0)
    second_ref[proj_ref.shape[0] - W_FIRST :] = jnp.where(
        line == 0, wts[0:1], jnp.where(line == 1, wts[1:2], 0.0)
    ).astype(BF16)
    count = SHARDS * SEG
    key_all = first_ref[:, :SEG].reshape(count, HEAD_SIZE)
    value_all = first_ref[:, SEG : 2 * SEG].reshape(count, HEAD_SIZE)
    scores = lax.dot_general(
        query_ref[...], key_all, (((1,), (1,)), ((), ())), preferred_element_type=F32
    ) * (1.0 / math.sqrt(HEAD_SIZE))
    row = lax.broadcasted_iota(jnp.int32, scores.shape, 0) + ctx_ref[0] * SEG
    visible = row >= lax.broadcasted_iota(jnp.int32, scores.shape, 1)
    scores = jnp.where(visible, scores, -1e30)
    weights = jnp.where(visible, jnp.exp(scores - jnp.max(scores, axis=1, keepdims=True)), 0.0)
    total = jnp.sum(weights, axis=1, keepdims=True)
    attn = jnp.dot(weights.astype(BF16), value_all, preferred_element_type=F32)
    gains = three_terms(jnp.broadcast_to(gain_ref[...], (EXTRA, HEAD_SIZE)))
    gain_rows = jnp.zeros((EXTRA, HEAD_SIZE), F32)
    for k in range(3):
        gain_rows = jnp.where(line == k, gains[k].astype(F32), gain_rows)
    sent = jnp.concatenate([(attn / total).astype(BF16), gain_rows.astype(BF16)], axis=0)
    out_ref[...] = jnp.broadcast_to(sent[None], out_ref.shape)


def attention(ctx_rank, queries, first, gain, wts, out_proj):
    return pl.pallas_call(
        attention_kernel,
        out_shape=[
            jax.ShapeDtypeStruct((QUERY_HEAD_COUNT, SEG + EXTRA, HEAD_SIZE), BF16),
            jax.ShapeDtypeStruct((out_proj.shape[0] - W_FIRST + EXTRA, HEAD_SIZE), BF16),
        ],
        in_specs=[SMEM] + [VMEM] * 5,
        out_specs=[VMEM, VMEM],
        compiler_params=pltpu.CompilerParams(vmem_limit_bytes=ATTENTION_ROOM),
    )(ctx_rank, queries, first, gain, wts, out_proj)


def project_kernel(
    ctx_ref, heads_ref, first_ref, second_ref, residual_ref, place_ref,
    out_ref, picked_ref, gain_ref, attn_v, proj_v,
):
    for h in range(QUERY_HEAD_COUNT):
        attn_v[:, h * 128 : (h + 1) * 128] = heads_ref[h, :SEG]
        gain_ref[:, h * 128 : (h + 1) * 128] = jnp.sum(
            heads_ref[h, SEG:].astype(F32), axis=0, keepdims=True
        )
    for c in range(SHARDS):
        proj_v[c * 256 : c * 256 + W_FIRST] = first_ref[c, 2 * SEG : 2 * SEG + W_FIRST]
        proj_v[c * 256 + W_FIRST : (c + 1) * 256] = second_ref[c, : 256 - W_FIRST]
    residual = residual_ref[...].astype(F32) + jnp.dot(
        attn_v[...], proj_v[...], preferred_element_type=F32
    )
    rounded = residual.astype(BF16)
    out_ref[...] = rounded
    line = lax.broadcasted_iota(jnp.int32, (EXPERTS * CAP, SEG), 0)
    place = place_ref[ctx_ref[0]]
    chosen = jnp.where((line == place[0:1]) | (line == place[1:2]), 1.0, 0.0)
    picked_ref[...] = jnp.dot(chosen.astype(BF16), rounded, preferred_element_type=F32).astype(BF16)


def project(ctx_rank, heads, first, second, residual_in, place):
    return pl.pallas_call(
        project_kernel,
        out_shape=[
            jax.ShapeDtypeStruct((SEG, 128), BF16),
            jax.ShapeDtypeStruct((EXPERTS * CAP, 128), BF16),
            jax.ShapeDtypeStruct((1, D), F32),
        ],
        in_specs=[SMEM] + [VMEM] * 5,
        out_specs=[VMEM] * 3,
        scratch_shapes=[pltpu.VMEM((SEG, D), BF16), pltpu.VMEM((D, 128), BF16)],
        compiler_params=pltpu.CompilerParams(vmem_limit_bytes=ATTENTION_ROOM),
    )(ctx_rank, heads, first, second, residual_in, place)


def after_kernel(near_ref, far_ref, other_ref, near_out, far_out):
    del near_ref, far_ref, other_ref, near_out, far_out


def after(near, far, other):
    return pl.pallas_call(
        after_kernel,
        out_shape=[jax.ShapeDtypeStruct(v.shape, v.dtype) for v in (near, far)],
        in_specs=[ANY, ANY, ANY],
        out_specs=[ANY, ANY],
        input_output_aliases={0: 0, 1: 1},
        compiler_params=pltpu.CompilerParams(vmem_limit_bytes=ROOM),
    )(near, far, other)


def experts_kernel(x_ref, *refs):
    weights, (out_ref, held_v, hidden_v, sems) = refs[:4], refs[4:]
    copies = []
    for part in range(2):
        for i in range(4):
            rows = pl.ds(part * 2 * D, 2 * D if part == 0 else D)
            copies.append(
                pltpu.make_async_copy(weights[i].at[rows], held_v.at[i, rows], sems.at[i, part])
            )
    for copy in copies:
        copy.start()
    x = x_ref[...]
    for i in range(4):
        copies[i].wait()
        both = jnp.dot(
            x,
            jnp.concatenate([held_v[i, :D], held_v[i, D : 2 * D]], axis=1),
            preferred_element_type=F32,
        )
        gate_val, up_val = both[:, :128], both[:, 128:]
        hidden_v[:, i * 128 : (i + 1) * 128] = (
            gate_val / (1.0 + jnp.exp(-gate_val)) * up_val
        ).astype(BF16)
    for i in range(4):
        copies[4 + i].wait()
    hidden = hidden_v[...]
    for b in range(0, D // 128, 2):
        start = 2 * D + b * 128
        down = jnp.concatenate(
            [
                jnp.concatenate(
                    [held_v[i, start : start + 128], held_v[i, start + 128 : start + 256]], axis=1
                )
                for i in range(4)
            ],
            axis=0,
        )
        part = jnp.dot(hidden, down, preferred_element_type=F32).astype(BF16)
        out_ref[b] = part[:, :128]
        out_ref[b + 1] = part[:, 128:]


def run_experts(rows_all, weights):
    rows = rows_all.shape[0]
    return pl.pallas_call(
        experts_kernel,
        out_shape=jax.ShapeDtypeStruct((D // 128, rows, 128), BF16),
        in_specs=[VMEM] + [ANY] * 4,
        out_specs=VMEM,
        scratch_shapes=[
            pltpu.VMEM((4, 3 * D, 128), BF16),
            pltpu.VMEM((rows, 512), BF16),
            pltpu.SemaphoreType.DMA((4, 2)),
        ],
        compiler_params=pltpu.CompilerParams(vmem_limit_bytes=ROOM),
        cost_estimate=pl.CostEstimate(
            flops=2 * rows * 512 * D * 3, bytes_accessed=12 * 128 * D * 2, transcendentals=0
        ),
    )(rows_all, *weights)


def weigh_kernel(parts_ref, combine_ref, out_ref):
    for g in range(SHARDS // 4):
        rows = parts_ref[:, g * 16 : (g + 1) * 16].reshape(QUERY_HEAD_COUNT * 16, 128)
        total = jnp.dot(combine_ref[g], rows, preferred_element_type=F32)
        out_ref[g * 4 : (g + 1) * 4] = total.astype(BF16).reshape(4, SEG, 128)


def weigh(parts, combine):
    return pl.pallas_call(
        weigh_kernel,
        out_shape=jax.ShapeDtypeStruct((SHARDS, SEG, 128), BF16),
        in_specs=[VMEM] * 2,
        out_specs=VMEM,
        compiler_params=pltpu.CompilerParams(vmem_limit_bytes=16 * 1024 * 1024),
    )(parts, combine)


def per_device(
    queries, keys, values, out_proj, residual_in, norm_gain, routes, gate_wts, w_gate, w_up, w_down
):
    ctx_count = lax.axis_size("ctx")
    exp_count = lax.axis_size("exp")
    ctx_rank = lax.axis_index("ctx")
    exp_rank = lax.axis_index("exp")
    rows_dev = CAP // (exp_count // EXPERTS)
    pair = [(i, i ^ 1) for i in range(exp_count)]
    chip = [(i, i ^ 2) for i in range(exp_count)]

    ctx = ctx_rank.astype(jnp.int32).reshape(1)

    head = (exp_rank // (QUERY_HEAD_COUNT // KEY_VALUE_HEADS)).astype(jnp.int32).reshape(1)
    near, sent = pack(head, w_gate, w_up, w_down, keys, values, out_proj)
    far = lax.ppermute(near, "exp", chip)

    first = lax.all_gather(sent, "ctx", axis=0)
    spread, rest = attention(
        ctx,
        queries,
        first,
        norm_gain.reshape(1, -1),
        gate_wts.T,
        out_proj,
    )
    heads = lax.all_to_all(spread, "exp", 0, 0)
    second = lax.all_gather(rest, "ctx", axis=0)
    gate_all = second[:, -EXTRA : TOP - EXTRA, :SEG]

    place = slot_places(routes.reshape(ctx_count, SEG, TOP))
    shard = jnp.arange(ctx_count, dtype=jnp.int32)[:, None, None] % 4
    column = (place // rows_dev) * 16 + shard * rows_dev + place % rows_dev
    columns = jnp.arange(exp_count * 16, dtype=jnp.int32)
    combine = sum(
        jnp.where(column[:, :, k, None] == columns, gate_all[:, k, :, None], jnp.zeros((), BF16))
        for k in range(TOP)
    ).reshape(ctx_count // 4, 4 * SEG, exp_count * 16)

    residual_out, picked, gain_all = project(
        ctx, heads, first, second, residual_in, place.transpose(0, 2, 1)
    )
    near, far = after(near, far, residual_out)
    across = lax.ppermute(near, "exp", pair)
    across_far = lax.ppermute(far, "exp", pair)

    mine = lax.all_to_all(picked.reshape(exp_count, rows_dev, -1), "exp", 0, 0)
    mine = mine.transpose(1, 0, 2).reshape(rows_dev, D).astype(F32)
    sq_mean = jnp.mean(mine * mine, axis=1, keepdims=True)
    normed = (mine * lax.rsqrt(sq_mean + 1e-05) * gain_all).astype(BF16)
    rows_all = lax.all_gather(normed, "ctx", axis=0).reshape(ctx_count * rows_dev, D)

    out = run_experts(rows_all, [near, across, far, across_far])

    parts = lax.all_to_all(out, "exp", 0, 0)
    pieces = lax.all_to_all(weigh(parts, combine), "ctx", 0, 0)
    expert_out = pieces.astype(F32).sum(axis=0).astype(BF16)
    return (residual_out, expert_out)


def solution(mesh):
    placed = (
        P("ctx", "exp"),
        P("ctx", None),
        P("ctx", None),
        P("ctx", "exp"),
        P("ctx", "exp"),
        P("exp"),
        P(),
        P("ctx", None),
        P(None, ("exp", "ctx")),
        P(None, ("exp", "ctx")),
        P(("exp", "ctx"), None),
    )
    return jax.shard_map(
        per_device,
        mesh=mesh,
        in_specs=placed,
        out_specs=(P("ctx", "exp"), P("ctx", "exp")),
        check_vma=False,
    )
```
